32 devices in a mesh: phase: 4 (over z), rows: 8 (over y, x, core).
Axes of the slice: x: 2, y: 2, z: 4, core: 2. Of those that a mesh axis runs over, the one named last changes fastest.
Arguments:
- start: bfloat16 [4, 8192, 256], P('phase', 'rows')
- blocks: bfloat16 [4, 64, 4, 128, 128], P('phase', 'rows')
- cols: int32 [4, 64, 4], P('phase', 'rows'), may hold values from 0 to 63, as said below
- counts: int32 [4, 64], P('phase', 'rows'), may hold values from 1 to 4, as said below
Outputs:
- basis: float32 [4, 8192, 256], P('phase', 'rows')
- factor: float32 [4, 256, 256], P('phase')
The draws below stay inside these ranges and needn't reach their ends.
Inputs may be any that keep to these rules, and one draw needn't show every extreme that they name: cols[q, i, 0] = i; the other slots of block row i name distinct block rows (i + o) mod 64 with 1 <= |o| <= 2. Block row i of section q uses its first counts[q, i] slots; every section has a block row that uses all 4.
All inputs are finite; a program needn't handle non-finite values.
Results may differ from the reference program's by a relative error of at most 0.012.
Values may be sent and summed in bfloat16 or wider, within the bound.
A program may use at most 64 MiB of HBM per device.

```python
import jax
import jax.numpy as jnp
from jax import lax

BS = 128
K = 256
HB = 2
MAXB = 4
PHASES = 4
NBR = 64
STATES = 8192


def draw_start(key, part):
    key_a = jax.random.fold_in(jax.random.fold_in(key, 3), 0)
    row_index = jnp.arange(STATES, dtype=jnp.float32)
    row_rise = jnp.exp(jnp.log(3.0) * row_index / STATES)[None, :, None]
    values = jnp.clip(jax.random.normal(key_a, (PHASES, STATES, K), jnp.float32), -5.0, 5.0) * row_rise
    return values.astype(jnp.bfloat16)


def draw_blocks(key, part):
    key_a, key_b = jax.random.split(jax.random.fold_in(key, 11), 2)
    shape = (PHASES, NBR, MAXB, BS, BS)
    spread = 0.5 / jnp.sqrt(jnp.float32(BS * MAXB))
    noise_part = jnp.clip(jax.random.normal(key_a, shape, jnp.float32), -4.0, 4.0) * spread
    diagonal_scale = jnp.exp(jax.random.uniform(key_b, (PHASES, NBR, 1, BS, 1), jnp.float32, jnp.log(0.6), jnp.log(1.6)))
    identity_mask = jnp.arange(BS)[:, None] == jnp.arange(BS)[None, :]
    first_slot = (jnp.arange(MAXB) == 0)[:, None, None]
    diagonal_part = jnp.where(identity_mask[None, None, None, :, :] & first_slot[None, None, :, :, :], diagonal_scale, 0.0)
    return (noise_part + diagonal_part).astype(jnp.bfloat16)


def draw_cols(key, part):
    key_a = jax.random.fold_in(key, 5)
    scores = jax.random.randint(key_a, (PHASES, NBR, 2 * HB), 0, 2 ** 20) * (2 * HB) + jnp.arange(2 * HB, dtype=jnp.int32)
    chosen = jnp.argsort(scores, axis=-1, stable=True)[:, :, :MAXB - 1].astype(jnp.int32)
    offsets = jnp.where(chosen < HB, chosen - HB, chosen - HB + 1)
    row_index = jnp.arange(NBR, dtype=jnp.int32)[None, :, None]
    others = jnp.mod(row_index + offsets, NBR)
    diagonal_col = jnp.broadcast_to(row_index, (PHASES, NBR, 1))
    return jnp.concatenate([diagonal_col, others], axis=-1).astype(jnp.int32)


def draw_counts(key, part):
    key_a, key_b = jax.random.split(jax.random.fold_in(key, 7), 2)
    base_draw = jax.random.randint(key_a, (PHASES, NBR), 1, MAXB + 1)
    full_row = jax.random.randint(key_b, (PHASES, 1), 0, NBR)
    row_index = jnp.arange(NBR, dtype=jnp.int32)[None, :]
    return jnp.where(row_index == full_row, MAXB, base_draw).astype(jnp.int32)


def setup_inputs(seed: int = 0) -> dict:
    streams_of = jax.random.split(jax.random.key(seed), 5)
    start = draw_start(jax.random.fold_in(streams_of[4], 71), 0)
    blocks = draw_blocks(jax.random.fold_in(streams_of[4], 71), 0)
    cols = draw_cols(jax.random.fold_in(streams_of[4], 71), 0)
    counts = draw_counts(jax.random.fold_in(streams_of[4], 71), 0)
    return {"start": start, "blocks": blocks, "cols": cols, "counts": counts}


def section_apply(section_item):
    section_blocks, section_cols, section_counts, travel = section_item
    row_tiles = travel.reshape(STATES // BS, BS, K)
    picked = row_tiles[section_cols].astype(jnp.float32)
    live_slots = jnp.arange(MAXB, dtype=jnp.int32)[None, :] < section_counts[:, None]
    kept_blocks = jnp.where(live_slots[:, :, None, None], section_blocks.astype(jnp.float32), jnp.float32(0.0))
    applied = jnp.einsum('ijab,ijbk->iak', kept_blocks, picked)
    return applied.reshape(STATES, K).astype(jnp.bfloat16)

def finish(travel):
    gram_term = jnp.dot(travel.T.astype(jnp.float32), travel.astype(jnp.float32), preferred_element_type=jnp.float32)
    gram_matrix = gram_term / STATES
    lower_factor = jnp.linalg.cholesky(gram_matrix)
    basis_out = jax.scipy.linalg.solve_triangular(lower_factor, travel.astype(jnp.float32).T, lower=True).T
    return (basis_out, lower_factor.T)

def reference(start, blocks, cols, counts):

    def advance(travel, offset_turn):
        aligned = jnp.roll(travel, offset_turn, axis=0)
        applied = lax.map(section_apply, (blocks, cols, counts, aligned))
        return (jnp.roll(applied, -offset_turn, axis=0), jnp.int32(0))
    arrived, unused = lax.scan(advance, start, jnp.arange(PHASES, dtype=jnp.int32))
    basis, factor = lax.map(finish, arrived)
    return (basis, factor)
```

```python
import functools

import jax
import jax.numpy as jnp
from jax import lax
from jax.experimental import pallas as pl
from jax.experimental.pallas import tpu as pltpu
from jax.sharding import PartitionSpec as P

HB = 2
LANES = 128
MESH = pl.DeviceIdType.MESH


def when(condition):
    if condition is True:
        return lambda f: f()
    if condition is False:
        return lambda f: None
    return pl.when(condition)


def travel_kernel(
    phases, owners, reducers,
    start_ref, blocks_ref, cols_ref, counts_ref,
    arrived_ref, gram_ref,
    band, ext, prod, terms, inbox, piece, whole,
    halo_send, halo_recv, z_send, z_recv, rs_send, rs_recv, ag_send, ag_recv,
):
    block_rows, slots, tile, _ = blocks_ref.shape
    rows_here, width = start_ref.shape
    panels = width // LANES
    rim = HB * tile
    reach = 2 * HB + 1
    total_blocks = block_rows * owners
    me_z = lax.axis_index("phase")
    me = lax.axis_index("rows")
    nxt = lax.rem(me_z + 1, phases)
    prv = lax.rem(me_z + phases - 1, phases)
    right = lax.rem(me + 1, owners)
    left = lax.rem(me + owners - 1, owners)

    barrier = pltpu.get_barrier_semaphore()
    for z in (nxt, prv):
        pl.semaphore_signal(barrier, inc=1, device_id=(z, me), device_id_type=MESH)

    def greet(d, carry):
        pl.semaphore_signal(
            barrier, inc=1, device_id=(me_z, lax.rem(me + d, owners)), device_id_type=MESH
        )
        return carry

    lax.fori_loop(1, owners, greet, 0)
    for c in range(panels):
        ext[0, c, rim : rim + rows_here, :] = start_ref[:, c * LANES : (c + 1) * LANES]
    pl.semaphore_wait(barrier, owners - 1 + 2)

    own = (0, rim, rows_here)
    parts = [(0, rim), (rows_here - rim, rim)]
    if rows_here > 2 * rim:
        parts.append((rim, rows_here - 2 * rim))

    waits = []

    def send_halo(s, c, side):
        source = rim if side == 0 else rows_here
        target = rim + rows_here if side == 0 else 0
        copy = pltpu.make_async_remote_copy(
            src_ref=ext.at[s, c, pl.ds(source, rim), :],
            dst_ref=ext.at[s, c, pl.ds(target, rim), :],
            send_sem=halo_send.at[s, c, side],
            recv_sem=halo_recv.at[s, c, side],
            device_id=(me_z, left if side == 0 else right),
            device_id_type=MESH,
        )
        copy.start()
        waits.append(copy)
        return copy

    def z_copy(s, c, k):
        at, size = parts[k]
        return pltpu.make_async_remote_copy(
            src_ref=prod.at[s, c, pl.ds(at, size), :],
            dst_ref=ext.at[s + 1, c, pl.ds(rim + at, size), :],
            send_sem=z_send.at[s, c, k],
            recv_sem=z_recv.at[s, c, k],
            device_id=(nxt, me),
            device_id_type=MESH,
        )

    def multiply(s, c, i):
        prod[s, c, i * tile : (i + 1) * tile, :] = jnp.dot(
            band[i], ext[s, c, i * tile : (i + reach) * tile, :], preferred_element_type=jnp.float32
        ).astype(jnp.bfloat16)

    halos = {}
    for c in range(panels):
        for side in range(2):
            halos[0, c, side] = send_halo(0, c, side)

    nothing = jnp.zeros((tile, tile), jnp.bfloat16)
    for i in range(block_rows):
        row = me * block_rows + i
        band[i, :, HB * tile : (HB + 1) * tile] = blocks_ref[i, 0]
        for o in range(reach):
            if o == HB:
                continue
            column = lax.rem(row + (o - HB) + total_blocks, total_blocks)
            kept = nothing
            for j in range(1, slots):
                live = (cols_ref[i, j] == column) & (j < counts_ref[i])
                kept = lax.select(live, blocks_ref[i, j], kept)
            band[i, :, o * tile : (o + 1) * tile] = kept

    for s in range(phases):
        for c in range(panels):
            if s > 0:
                for k in range(2):
                    z_copy(s - 1, c, k).wait_recv()
                    halos[s, c, k] = send_halo(s, c, k)
                for k in range(2, len(parts)):
                    z_copy(s - 1, c, k).wait_recv()
            for side in range(2):
                halos[s, c, side].wait_recv()
            for k, (at, size) in enumerate(parts):
                for i in range(at // tile, (at + size) // tile):
                    multiply(s, c, i)
                copy = z_copy(s, c, k)
                copy.start()
                waits.append(copy)

    rows = (rim, rim + rows_here)
    share = width // reducers
    contract = (((0,), (0,)), ((), ()))
    for c in range(panels):
        for k in range(len(parts)):
            z_copy(phases - 1, c, k).wait_recv()
        arrived_ref[:, c * LANES : (c + 1) * LANES] = ext[phases, c, rows[0] : rows[1], :]
    arrived = arrived_ref[...]
    gram = lax.dot_general(arrived, arrived, contract, preferred_element_type=jnp.float32)
    terms[...] = gram.astype(jnp.bfloat16).reshape(reducers, share, width)

    few = owners > reducers
    i_reduce = (me < reducers) if few else True

    def rs_copy(d):
        to = lax.rem(me + d, owners)
        return pltpu.make_async_remote_copy(
            src_ref=terms.at[lax.rem(to, reducers)],
            dst_ref=inbox.at[d],
            send_sem=rs_send.at[d],
            recv_sem=rs_recv.at[d],
            device_id=(me_z, to),
            device_id_type=MESH,
        ), ((to < reducers) if few else True)

    def ag_copy(d):
        to = lax.rem(me + d, owners)
        return pltpu.make_async_remote_copy(
            src_ref=piece,
            dst_ref=whole.at[lax.rem(me, reducers)],
            send_sem=ag_send.at[d],
            recv_sem=ag_recv.at[d],
            device_id=(me_z, to),
            device_id_type=MESH,
        )

    def ag_arrival(d):
        frm = lax.rem(me + owners - d, owners)
        return pltpu.make_async_remote_copy(
            src_ref=piece,
            dst_ref=whole.at[lax.rem(frm, reducers)],
            send_sem=ag_send.at[d],
            recv_sem=ag_recv.at[d],
            device_id=(me_z, frm),
            device_id_type=MESH,
        ), ((frm < reducers) if few else True)

    for d in range(1, owners):
        copy, to_reducer = rs_copy(d)
        when(to_reducer)(copy.start)

    def reduce_piece():
        total = terms[lax.rem(me, reducers)].astype(jnp.float32)
        for d in range(1, owners):
            rs_copy(d)[0].wait_recv()
            total = total + inbox[d].astype(jnp.float32)
        total = total * (1.0 / (rows_here * owners))
        piece[...] = total
        for d in range(1, owners):
            ag_copy(d).start()
        whole[lax.rem(me, reducers)] = total

    when(i_reduce)(reduce_piece)
    for d in range(1, owners):
        copy, from_reducer = ag_arrival(d)
        when(from_reducer)(copy.wait_recv)
    gram_ref[...] = whole[...].reshape(width, width)

    for copy in waits:
        copy.wait_send()
    for d in range(1, owners):
        copy, to_reducer = rs_copy(d)
        when(to_reducer)(copy.wait_send)

    def sent():
        for d in range(1, owners):
            ag_copy(d).wait_send()

    when(i_reduce)(sent)


def travel(start, blocks, cols, counts):
    block_rows, slots, tile, _ = blocks.shape
    rows_here, width = start.shape
    phases, owners = lax.axis_size("phase"), lax.axis_size("rows")
    panels = width // LANES
    rim = HB * tile
    reducers = min(owners, width // 32)
    share = width // reducers
    part_count = 3 if rows_here > 2 * rim else 2
    dma = pltpu.SemaphoreType.DMA
    vmem = pl.BlockSpec(memory_space=pltpu.VMEM)
    smem = pl.BlockSpec(memory_space=pltpu.SMEM)
    return pl.pallas_call(
        functools.partial(travel_kernel, phases, owners, reducers),
        out_shape=(
            jax.ShapeDtypeStruct((rows_here, width), jnp.bfloat16),
            jax.ShapeDtypeStruct((width, width), jnp.float32),
        ),
        in_specs=[vmem, vmem, smem, smem],
        out_specs=(vmem, vmem),
        scratch_shapes=[
            pltpu.VMEM((block_rows, tile, (2 * HB + 1) * tile), jnp.bfloat16),
            pltpu.VMEM((phases + 1, panels, rows_here + 2 * rim, LANES), jnp.bfloat16),
            pltpu.VMEM((phases, panels, rows_here, LANES), jnp.bfloat16),
            pltpu.VMEM((reducers, share, width), jnp.bfloat16),
            pltpu.VMEM((owners, share, width), jnp.bfloat16),
            pltpu.VMEM((share, width), jnp.float32),
            pltpu.VMEM((reducers, share, width), jnp.float32),
            dma((phases, panels, 2)),
            dma((phases, panels, 2)),
            dma((phases, panels, part_count)),
            dma((phases, panels, part_count)),
            dma((owners,)),
            dma((owners,)),
            dma((owners,)),
            dma((owners,)),
        ],
        compiler_params=pltpu.CompilerParams(
            collective_id=0, has_side_effects=True, vmem_limit_bytes=48 * 1024 * 1024
        ),
        name="travel",
    )(start, blocks, cols, counts)


def ortho_kernel(panel, gram_ref, arrived_ref, basis_ref, factor_ref, upper, inverse):
    n = gram_ref.shape[0]
    leaf = 8
    row_at = lax.broadcasted_iota(jnp.int32, (n, n), 0)
    col_at = lax.broadcasted_iota(jnp.int32, (n, n), 1)
    upper[...] = gram_ref[...]
    inverse[...] = jnp.where(row_at == col_at, 1.0, 0.0).astype(jnp.float32)
    at_row = lax.broadcasted_iota(jnp.int32, (leaf, LANES), 0)

    for first in range(0, n, panel):
        lo = first // LANES * LANES
        hi = ((first + panel - 1) // LANES + 1) * LANES
        places = [(upper, t) for t in range(lo, n, LANES)] + [(inverse, t) for t in range(0, hi, LANES)]
        rest = [ref[first : first + panel, t : t + LANES] for ref, t in places]
        for base in range(first, first + panel, leaf):
            left = first + panel - base - leaf
            heads = [x[:leaf] for x in rest]
            tails = [x[leaf:] for x in rest] if left else []
            pick = base % LANES
            source = (base // LANES * LANES - lo) // LANES
            col_head = [
                jnp.broadcast_to(heads[source][:, pick + j : pick + j + 1], (leaf, LANES)) for j in range(leaf)
            ]
            col_tail = [
                jnp.broadcast_to(tails[source][:, pick + j : pick + j + 1], (left, LANES)) for j in range(leaf)
            ] if left else []
            for k in range(leaf):
                scale = lax.rsqrt(col_head[k][k : k + 1, :])
                low = col_head[k] * scale
                low_tail = col_tail[k] * scale if left else None
                for j in range(k + 1, leaf):
                    by = low[j : j + 1, :]
                    col_head[j] = col_head[j] - low * by
                    if left:
                        col_tail[j] = col_tail[j] - low_tail * by
                masked = jnp.where(at_row > k, low, 0.0)
                for t in range(len(places)):
                    row = heads[t][k : k + 1, :] * scale
                    heads[t] = jnp.where(at_row == k, row, heads[t] - masked * row)
                    if left:
                        tails[t] = tails[t] - low_tail * row
            for (ref, t), head in zip(places, heads):
                ref[base : base + leaf, t : t + LANES] = head
            rest = tails
        done = first + panel
        if done < n:
            start = done // LANES * LANES
            solved = upper[first:done, start:]
            contract = (((0,), (0,)), ((), ()))
            for ref, a, b in ((upper, start, n), (inverse, 0, hi)):
                change = lax.dot_general(
                    solved, ref[first:done, a:b], contract,
                    precision=lax.Precision.HIGHEST, preferred_element_type=jnp.float32,
                )
                ref[done:, a:b] = ref[done:, a:b] - change[done - start :]
    factor_ref[...] = jnp.where(col_at >= row_at, upper[...], 0.0)
    weights = inverse[...]
    coarse = weights.astype(jnp.bfloat16)
    fine = (weights - coarse.astype(jnp.float32)).astype(jnp.bfloat16)
    contract = (((1,), (1,)), ((), ()))
    step = n
    for at in range(0, arrived_ref.shape[0], step):
        rows = arrived_ref[at : at + step, :]
        basis_ref[at : at + step, :] = lax.dot_general(
            rows, coarse, contract, preferred_element_type=jnp.float32
        ) + lax.dot_general(rows, fine, contract, preferred_element_type=jnp.float32)


def ortho(gram, arrived, panel=32):
    n = gram.shape[0]
    vmem = pl.BlockSpec(memory_space=pltpu.VMEM)
    return pl.pallas_call(
        functools.partial(ortho_kernel, panel),
        out_shape=(
            jax.ShapeDtypeStruct(arrived.shape, jnp.float32),
            jax.ShapeDtypeStruct((n, n), jnp.float32),
        ),
        in_specs=[vmem, vmem],
        out_specs=(vmem, vmem),
        scratch_shapes=[pltpu.VMEM((n, n), jnp.float32)] * 2,
        compiler_params=pltpu.CompilerParams(vmem_limit_bytes=32 * 1024 * 1024),
        name="ortho",
    )(gram, arrived)


def body(start, blocks, cols, counts):
    arrived, gram = travel(start[0], blocks[0], cols[0], counts[0])
    basis, factor = ortho(gram, arrived)
    return (basis[None], factor[None])


def solution(mesh):
    placed = (
        P("phase", "rows", None),
        P("phase", "rows", None, None, None),
        P("phase", "rows", None),
        P("phase", "rows"),
    )
    return jax.shard_map(
        body,
        mesh=mesh,
        in_specs=placed,
        out_specs=(P("phase", "rows", None), P("phase", None, None)),
        check_vma=False,
    )
```

```python
import functools

import jax
import jax.numpy as jnp
from jax import lax
from jax.experimental import pallas as pl
from jax.experimental.pallas import tpu as pltpu
from jax.sharding import PartitionSpec as P

HB = 2
LANES = 128
MESH = pl.DeviceIdType.MESH


def when(condition):
    if condition is True:
        return lambda f: f()
    if condition is False:
        return lambda f: None
    return pl.when(condition)


def travel_kernel(
    phases, owners, reducers,
    start_ref, blocks_ref, cols_ref, counts_ref,
    arrived_ref, gram_ref,
    tiles, band, ext, prod, terms, inbox, piece, landed, whole,
    load, halo_send, halo_recv, z_send, z_recv, rs_send, rs_recv, hop_send, hop_recv, ag_send, ag_recv,
):
    block_rows, slots, tile, _ = blocks_ref.shape
    rows_here, width = start_ref.shape
    panels = width // LANES
    rim = HB * tile
    reach = 2 * HB + 1
    total_blocks = block_rows * owners
    me_z = lax.axis_index("phase")
    me = lax.axis_index("rows")
    nxt = lax.rem(me_z + 1, phases)
    prv = lax.rem(me_z + phases - 1, phases)
    right = lax.rem(me + 1, owners)
    left = lax.rem(me + owners - 1, owners)

    loads = [
        pltpu.make_async_copy(
            start_ref.at[:, pl.ds(c * LANES, LANES)], ext.at[0, c, pl.ds(rim, rows_here), :], load.at[c]
        )
        for c in range(panels)
    ]
    loads.append(pltpu.make_async_copy(blocks_ref, tiles, load.at[panels]))
    for copy in reversed(loads):
        copy.start()

    barrier = pltpu.get_barrier_semaphore()
    for z in (nxt, prv):
        pl.semaphore_signal(barrier, inc=1, device_id=(z, me), device_id_type=MESH)

    def greet(d, carry):
        pl.semaphore_signal(
            barrier, inc=1, device_id=(me_z, lax.rem(me + d, owners)), device_id_type=MESH
        )
        return carry

    lax.fori_loop(1, owners, greet, 0)
    loads[panels].wait()

    nothing = jnp.zeros((tile, tile), jnp.bfloat16)
    for i in range(block_rows):
        row = me * block_rows + i
        band[i, :, HB * tile : (HB + 1) * tile] = tiles[i, 0]
        for o in range(reach):
            if o == HB:
                continue
            column = lax.rem(row + (o - HB) + total_blocks, total_blocks)
            kept = nothing
            for j in range(1, slots):
                live = (cols_ref[i, j] == column) & (j < counts_ref[i])
                kept = lax.select(live, tiles[i, j], kept)
            band[i, :, o * tile : (o + 1) * tile] = kept

    for copy in loads[:panels]:
        copy.wait()
    pl.semaphore_wait(barrier, owners - 1 + 2)

    parts = [(0, rim), (rows_here - rim, rim)]
    if rows_here > 2 * rim:
        parts.append((rim, rows_here - 2 * rim))

    waits = []

    def send_halo(s, c, side):
        source = rim if side == 0 else rows_here
        target = rim + rows_here if side == 0 else 0
        copy = pltpu.make_async_remote_copy(
            src_ref=ext.at[s, c, pl.ds(source, rim), :],
            dst_ref=ext.at[s, c, pl.ds(target, rim), :],
            send_sem=halo_send.at[s, c, side],
            recv_sem=halo_recv.at[s, c, side],
            device_id=(me_z, left if side == 0 else right),
            device_id_type=MESH,
        )
        copy.start()
        waits.append(copy)
        return copy

    def z_copy(s, c, k):
        at, size = parts[k]
        return pltpu.make_async_remote_copy(
            src_ref=prod.at[s, c, pl.ds(at, size), :],
            dst_ref=ext.at[s + 1, c, pl.ds(rim + at, size), :],
            send_sem=z_send.at[s, c, k],
            recv_sem=z_recv.at[s, c, k],
            device_id=(nxt, me),
            device_id_type=MESH,
        )

    def multiply(s, c, i):
        prod[s, c, i * tile : (i + 1) * tile, :] = jnp.dot(
            band[i], ext[s, c, i * tile : (i + reach) * tile, :], preferred_element_type=jnp.float32
        ).astype(jnp.bfloat16)

    halos = {}
    for c in range(panels):
        for side in range(2):
            halos[0, c, side] = send_halo(0, c, side)

    for s in range(phases):
        for c in range(panels):
            if s > 0:
                for k in range(2):
                    z_copy(s - 1, c, k).wait_recv()
                    halos[s, c, k] = send_halo(s, c, k)
                for k in range(2, len(parts)):
                    z_copy(s - 1, c, k).wait_recv()
            order = list(range(len(parts)))
            if s == 0 and c == 0:
                order = order[2:] + order[:2]
            rimmed = False
            for k in order:
                at, size = parts[k]
                if k < 2 and not rimmed:
                    for side in range(2):
                        halos[s, c, side].wait_recv()
                    rimmed = True
                for i in range(at // tile, (at + size) // tile):
                    multiply(s, c, i)
                copy = z_copy(s, c, k)
                copy.start()
                waits.append(copy)

    share = width // reducers
    contract = (((0,), (0,)), ((), ()))
    leaving = jnp.concatenate([prod[phases - 1, c] for c in range(panels)], axis=1)
    gram = lax.dot_general(leaving, leaving, contract, preferred_element_type=jnp.float32)
    terms[...] = gram.astype(jnp.bfloat16).reshape(reducers, share, width)

    few = owners > reducers
    i_reduce = (me < reducers) if few else True

    def rs_copy(d):
        to = lax.rem(me + d, owners)
        return pltpu.make_async_remote_copy(
            src_ref=terms.at[lax.rem(to, reducers)],
            dst_ref=inbox.at[d],
            send_sem=rs_send.at[d],
            recv_sem=rs_recv.at[d],
            device_id=(me_z, to),
            device_id_type=MESH,
        ), ((to < reducers) if few else True)

    hop = pltpu.make_async_remote_copy(
        src_ref=piece,
        dst_ref=landed,
        send_sem=hop_send.at[0],
        recv_sem=hop_recv.at[0],
        device_id=(nxt, me),
        device_id_type=MESH,
    )

    def ag_copy(d):
        to = lax.rem(me + d, owners)
        return pltpu.make_async_remote_copy(
            src_ref=landed,
            dst_ref=whole.at[lax.rem(me, reducers)],
            send_sem=ag_send.at[d],
            recv_sem=ag_recv.at[d],
            device_id=(me_z, to),
            device_id_type=MESH,
        )

    def ag_arrival(d):
        frm = lax.rem(me + owners - d, owners)
        return pltpu.make_async_remote_copy(
            src_ref=landed,
            dst_ref=whole.at[lax.rem(frm, reducers)],
            send_sem=ag_send.at[d],
            recv_sem=ag_recv.at[d],
            device_id=(me_z, frm),
            device_id_type=MESH,
        ), ((frm < reducers) if few else True)

    for d in range(1, owners):
        copy, to_reducer = rs_copy(d)
        when(to_reducer)(copy.start)

    def reduce_piece():
        total = terms[lax.rem(me, reducers)].astype(jnp.float32)
        for d in range(1, owners):
            rs_copy(d)[0].wait_recv()
            total = total + inbox[d].astype(jnp.float32)
        piece[...] = total * (1.0 / (rows_here * owners))
        hop.start()

    def spread_piece():
        hop.wait_recv()
        for d in range(1, owners):
            ag_copy(d).start()
        whole[lax.rem(me, reducers)] = landed[...]

    when(i_reduce)(reduce_piece)
    when(i_reduce)(spread_piece)
    stores = []
    for c in range(panels):
        for k in range(len(parts)):
            z_copy(phases - 1, c, k).wait_recv()
        store = pltpu.make_async_copy(
            ext.at[phases, c, pl.ds(rim, rows_here), :], arrived_ref.at[:, pl.ds(c * LANES, LANES)], load.at[c]
        )
        store.start()
        stores.append(store)
    for d in range(1, owners):
        copy, from_reducer = ag_arrival(d)
        when(from_reducer)(copy.wait_recv)
    gram_ref[...] = whole[...].reshape(width, width)

    for store in stores:
        store.wait()
    for copy in waits:
        copy.wait_send()
    for d in range(1, owners):
        copy, to_reducer = rs_copy(d)
        when(to_reducer)(copy.wait_send)

    def sent():
        hop.wait_send()
        for d in range(1, owners):
            ag_copy(d).wait_send()

    when(i_reduce)(sent)


def travel(start, blocks, cols, counts):
    block_rows, slots, tile, _ = blocks.shape
    rows_here, width = start.shape
    phases, owners = lax.axis_size("phase"), lax.axis_size("rows")
    panels = width // LANES
    rim = HB * tile
    reducers = min(owners, width // 32)
    share = width // reducers
    part_count = 3 if rows_here > 2 * rim else 2
    dma = pltpu.SemaphoreType.DMA
    vmem = pl.BlockSpec(memory_space=pltpu.VMEM)
    smem = pl.BlockSpec(memory_space=pltpu.SMEM)
    anywhere = pl.BlockSpec(memory_space=pl.ANY)
    return pl.pallas_call(
        functools.partial(travel_kernel, phases, owners, reducers),
        out_shape=(
            jax.ShapeDtypeStruct((rows_here, width), jnp.bfloat16),
            jax.ShapeDtypeStruct((width, width), jnp.float32),
        ),
        in_specs=[anywhere, anywhere, smem, smem],
        out_specs=(anywhere, vmem),
        scratch_shapes=[
            pltpu.VMEM((block_rows, slots, tile, tile), jnp.bfloat16),
            pltpu.VMEM((block_rows, tile, (2 * HB + 1) * tile), jnp.bfloat16),
            pltpu.VMEM((phases + 1, panels, rows_here + 2 * rim, LANES), jnp.bfloat16),
            pltpu.VMEM((phases, panels, rows_here, LANES), jnp.bfloat16),
            pltpu.VMEM((reducers, share, width), jnp.bfloat16),
            pltpu.VMEM((owners, share, width), jnp.bfloat16),
            pltpu.VMEM((share, width), jnp.float32),
            pltpu.VMEM((share, width), jnp.float32),
            pltpu.VMEM((reducers, share, width), jnp.float32),
            dma((panels + 1,)),
            dma((phases, panels, 2)),
            dma((phases, panels, 2)),
            dma((phases, panels, part_count)),
            dma((phases, panels, part_count)),
            dma((owners,)),
            dma((owners,)),
            dma((1,)),
            dma((1,)),
            dma((owners,)),
            dma((owners,)),
        ],
        compiler_params=pltpu.CompilerParams(
            collective_id=0, has_side_effects=True, vmem_limit_bytes=62 * 1024 * 1024
        ),
        name="travel",
    )(start, blocks, cols, counts)


def ortho_kernel(
    panel, gram_ref, arrived_hbm, basis_hbm, factor_ref, upper, inverse, arrived_ref, basis_ref, load, store
):
    n = gram_ref.shape[0]
    leaf = 8
    fetch = pltpu.make_async_copy(arrived_hbm, arrived_ref, load.at[0])
    fetch.start()
    row_at = lax.broadcasted_iota(jnp.int32, (n, n), 0)
    col_at = lax.broadcasted_iota(jnp.int32, (n, n), 1)
    upper[...] = gram_ref[...]
    inverse[...] = jnp.where(row_at == col_at, 1.0, 0.0).astype(jnp.float32)
    at_row = lax.broadcasted_iota(jnp.int32, (leaf, LANES), 0)

    for first in range(0, n, panel):
        lo = first // LANES * LANES
        hi = ((first + panel - 1) // LANES + 1) * LANES
        places = [(upper, t) for t in range(lo, n, LANES)] + [(inverse, t) for t in range(0, hi, LANES)]
        rest = [ref[first : first + panel, t : t + LANES] for ref, t in places]
        for base in range(first, first + panel, leaf):
            left = first + panel - base - leaf
            heads = [x[:leaf] for x in rest]
            tails = [x[leaf:] for x in rest] if left else []
            pick = base % LANES
            source = (base // LANES * LANES - lo) // LANES
            col_head = [
                jnp.broadcast_to(heads[source][:, pick + j : pick + j + 1], (leaf, LANES)) for j in range(leaf)
            ]
            col_tail = [
                jnp.broadcast_to(tails[source][:, pick + j : pick + j + 1], (left, LANES)) for j in range(leaf)
            ] if left else []
            for k in range(leaf):
                scale = lax.rsqrt(col_head[k][k : k + 1, :])
                low = col_head[k] * scale
                low_tail = col_tail[k] * scale if left else None
                for j in range(k + 1, leaf):
                    by = low[j : j + 1, :]
                    col_head[j] = col_head[j] - low * by
                    if left:
                        col_tail[j] = col_tail[j] - low_tail * by
                masked = jnp.where(at_row > k, low, 0.0)
                for t in range(len(places)):
                    row = heads[t][k : k + 1, :] * scale
                    heads[t] = jnp.where(at_row == k, row, heads[t] - masked * row)
                    if left:
                        tails[t] = tails[t] - low_tail * row
            for (ref, t), head in zip(places, heads):
                ref[base : base + leaf, t : t + LANES] = head
            rest = tails
        done = first + panel
        if done < n:
            start = done // LANES * LANES
            solved = upper[first:done, start:]
            contract = (((0,), (0,)), ((), ()))
            for ref, a, b in ((upper, start, n), (inverse, 0, hi)):
                change = lax.dot_general(
                    solved, ref[first:done, a:b], contract,
                    precision=lax.Precision.HIGHEST, preferred_element_type=jnp.float32,
                )
                ref[done:, a:b] = ref[done:, a:b] - change[done - start :]
    factor_ref[...] = jnp.where(col_at >= row_at, upper[...], 0.0)
    weights = inverse[...]
    coarse = weights.astype(jnp.bfloat16)
    fine = (weights - coarse.astype(jnp.float32)).astype(jnp.bfloat16)
    contract = (((1,), (1,)), ((), ()))
    step = n
    fetch.wait()
    writes = []
    for at in range(0, arrived_ref.shape[0], step):
        rows = arrived_ref[at : at + step, :]
        basis_ref[at : at + step, :] = lax.dot_general(
            rows, coarse, contract, preferred_element_type=jnp.float32
        ) + lax.dot_general(rows, fine, contract, preferred_element_type=jnp.float32)
        write = pltpu.make_async_copy(
            basis_ref.at[pl.ds(at, step), :], basis_hbm.at[pl.ds(at, step), :], store.at[at // step]
        )
        write.start()
        writes.append(write)
    for write in writes:
        write.wait()


def ortho(gram, arrived, panel=32):
    n = gram.shape[0]
    vmem = pl.BlockSpec(memory_space=pltpu.VMEM)
    return pl.pallas_call(
        functools.partial(ortho_kernel, panel),
        out_shape=(
            jax.ShapeDtypeStruct(arrived.shape, jnp.float32),
            jax.ShapeDtypeStruct((n, n), jnp.float32),
        ),
        in_specs=[vmem, pl.BlockSpec(memory_space=pl.ANY)],
        out_specs=(pl.BlockSpec(memory_space=pl.ANY), vmem),
        scratch_shapes=[
            pltpu.VMEM((n, n), jnp.float32),
            pltpu.VMEM((n, n), jnp.float32),
            pltpu.VMEM(arrived.shape, jnp.bfloat16),
            pltpu.VMEM(arrived.shape, jnp.float32),
            pltpu.SemaphoreType.DMA((1,)),
            pltpu.SemaphoreType.DMA((arrived.shape[0] // n,)),
        ],
        compiler_params=pltpu.CompilerParams(vmem_limit_bytes=62 * 1024 * 1024),
        name="ortho",
    )(gram, arrived)


def body(start, blocks, cols, counts):
    arrived, gram = travel(start[0], blocks[0], cols[0], counts[0])
    basis, factor = ortho(gram, arrived)
    return (basis[None], factor[None])


def solution(mesh):
    placed = (
        P("phase", "rows", None),
        P("phase", "rows", None, None, None),
        P("phase", "rows", None),
        P("phase", "rows"),
    )
    return jax.shard_map(
        body,
        mesh=mesh,
        in_specs=placed,
        out_specs=(P("phase", "rows", None), P("phase", None, None)),
        check_vma=False,
    )
```

```python
import functools

import jax
import jax.numpy as jnp
from jax import lax
from jax.experimental import pallas as pl
from jax.experimental.pallas import tpu as pltpu
from jax.sharding import PartitionSpec as P

HB = 2
LANES = 128
MESH = pl.DeviceIdType.MESH


def when(condition):
    if condition is True:
        return lambda f: f()
    if condition is False:
        return lambda f: None
    return pl.when(condition)


def travel_kernel(
    phases, owners, reducers,
    start_ref, blocks_ref, cols_ref, counts_ref,
    arrived_ref, gram_ref,
    tiles, band, ext, prod, terms, inbox, piece, landed, whole,
    load, halo_send, halo_recv, z_send, z_recv, rs_send, rs_recv, hop_send, hop_recv, ag_send, ag_recv,
):
    block_rows, slots, tile, _ = blocks_ref.shape
    rows_here, width = start_ref.shape
    panels = width // LANES
    rim = HB * tile
    reach = 2 * HB + 1
    total_blocks = block_rows * owners
    me_z = lax.axis_index("phase")
    me = lax.axis_index("rows")
    nxt = lax.rem(me_z + 1, phases)
    prv = lax.rem(me_z + phases - 1, phases)
    right = lax.rem(me + 1, owners)
    left = lax.rem(me + owners - 1, owners)

    loads = [
        pltpu.make_async_copy(
            start_ref.at[:, pl.ds(c * LANES, LANES)], ext.at[0, c, pl.ds(rim, rows_here), :], load.at[c]
        )
        for c in range(panels)
    ]
    loads.append(pltpu.make_async_copy(blocks_ref, tiles, load.at[panels]))
    for copy in reversed(loads):
        copy.start()

    barrier = pltpu.get_barrier_semaphore()
    for z in (nxt, prv):
        pl.semaphore_signal(barrier, inc=1, device_id=(z, me), device_id_type=MESH)

    def greet(d, carry):
        pl.semaphore_signal(
            barrier, inc=1, device_id=(me_z, lax.rem(me + d, owners)), device_id_type=MESH
        )
        return carry

    lax.fori_loop(1, owners, greet, 0)
    loads[panels].wait()

    nothing = jnp.zeros((tile, tile), jnp.bfloat16)
    for i in range(block_rows):
        row = me * block_rows + i
        band[i, :, HB * tile : (HB + 1) * tile] = tiles[i, 0]
        for o in range(reach):
            if o == HB:
                continue
            column = lax.rem(row + (o - HB) + total_blocks, total_blocks)
            kept = nothing
            for j in range(1, slots):
                live = (cols_ref[i, j] == column) & (j < counts_ref[i])
                kept = lax.select(live, tiles[i, j], kept)
            band[i, :, o * tile : (o + 1) * tile] = kept

    for copy in loads[:panels]:
        copy.wait()
    pl.semaphore_wait(barrier, owners - 1 + 2)

    parts = [(0, rim), (rows_here - rim, rim)]
    if rows_here > 2 * rim:
        parts.append((rim, rows_here - 2 * rim))

    waits = []

    def send_halo(s, c, side):
        source = rim if side == 0 else rows_here
        target = rim + rows_here if side == 0 else 0
        copy = pltpu.make_async_remote_copy(
            src_ref=ext.at[s, c, pl.ds(source, rim), :],
            dst_ref=ext.at[s, c, pl.ds(target, rim), :],
            send_sem=halo_send.at[s, c, side],
            recv_sem=halo_recv.at[s, c, side],
            device_id=(me_z, left if side == 0 else right),
            device_id_type=MESH,
        )
        copy.start()
        waits.append(copy)
        return copy

    def z_copy(s, c, k):
        at, size = parts[k]
        return pltpu.make_async_remote_copy(
            src_ref=prod.at[s, c, pl.ds(at, size), :],
            dst_ref=ext.at[s + 1, c, pl.ds(rim + at, size), :],
            send_sem=z_send.at[s, c, k],
            recv_sem=z_recv.at[s, c, k],
            device_id=(nxt, me),
            device_id_type=MESH,
        )

    def multiply(s, c, i):
        prod[s, c, i * tile : (i + 1) * tile, :] = jnp.dot(
            band[i], ext[s, c, i * tile : (i + reach) * tile, :], preferred_element_type=jnp.float32
        ).astype(jnp.bfloat16)

    halos = {}
    for c in range(panels):
        for side in range(2):
            halos[0, c, side] = send_halo(0, c, side)

    for s in range(phases):
        for c in range(panels):
            if s > 0:
                for k in range(2):
                    z_copy(s - 1, c, k).wait_recv()
                    halos[s, c, k] = send_halo(s, c, k)
                for k in range(2, len(parts)):
                    z_copy(s - 1, c, k).wait_recv()
            order = list(range(len(parts)))
            if s == 0 and c == 0:
                order = order[2:] + order[:2]
            rimmed = False
            for k in order:
                at, size = parts[k]
                if k < 2 and not rimmed:
                    for side in range(2):
                        halos[s, c, side].wait_recv()
                    rimmed = True
                for i in range(at // tile, (at + size) // tile):
                    multiply(s, c, i)
                copy = z_copy(s, c, k)
                copy.start()
                waits.append(copy)

    share = width // reducers
    contract = (((0,), (0,)), ((), ()))
    leaving = jnp.concatenate([prod[phases - 1, c] for c in range(panels)], axis=1)
    gram = lax.dot_general(leaving, leaving, contract, preferred_element_type=jnp.float32)
    terms[...] = gram.astype(jnp.bfloat16).reshape(reducers, share, width)

    few = owners > reducers
    i_reduce = (me < reducers) if few else True

    def rs_copy(d):
        to = lax.rem(me + d, owners)
        return pltpu.make_async_remote_copy(
            src_ref=terms.at[lax.rem(to, reducers)],
            dst_ref=inbox.at[d],
            send_sem=rs_send.at[d],
            recv_sem=rs_recv.at[d],
            device_id=(me_z, to),
            device_id_type=MESH,
        ), ((to < reducers) if few else True)

    hop = pltpu.make_async_remote_copy(
        src_ref=piece,
        dst_ref=landed,
        send_sem=hop_send.at[0],
        recv_sem=hop_recv.at[0],
        device_id=(nxt, me),
        device_id_type=MESH,
    )

    def ag_copy(d):
        to = lax.rem(me + d, owners)
        return pltpu.make_async_remote_copy(
            src_ref=landed,
            dst_ref=whole.at[lax.rem(me, reducers)],
            send_sem=ag_send.at[d],
            recv_sem=ag_recv.at[d],
            device_id=(me_z, to),
            device_id_type=MESH,
        )

    def ag_arrival(d):
        frm = lax.rem(me + owners - d, owners)
        return pltpu.make_async_remote_copy(
            src_ref=landed,
            dst_ref=whole.at[lax.rem(frm, reducers)],
            send_sem=ag_send.at[d],
            recv_sem=ag_recv.at[d],
            device_id=(me_z, frm),
            device_id_type=MESH,
        ), ((frm < reducers) if few else True)

    for d in range(1, owners):
        copy, to_reducer = rs_copy(d)
        when(to_reducer)(copy.start)

    def reduce_piece():
        total = terms[lax.rem(me, reducers)].astype(jnp.float32)
        for d in range(1, owners):
            rs_copy(d)[0].wait_recv()
            total = total + inbox[d].astype(jnp.float32)
        piece[...] = total * (1.0 / (rows_here * owners))
        hop.start()

    def spread_piece():
        hop.wait_recv()
        for d in range(1, owners):
            ag_copy(d).start()
        whole[lax.rem(me, reducers)] = landed[...]

    when(i_reduce)(reduce_piece)
    when(i_reduce)(spread_piece)
    stores = []
    for c in range(panels):
        for k in range(len(parts)):
            z_copy(phases - 1, c, k).wait_recv()
        store = pltpu.make_async_copy(
            ext.at[phases, c, pl.ds(rim, rows_here), :], arrived_ref.at[:, pl.ds(c * LANES, LANES)], load.at[c]
        )
        store.start()
        stores.append(store)
    for d in range(1, owners):
        copy, from_reducer = ag_arrival(d)
        when(from_reducer)(copy.wait_recv)
    gram_ref[...] = whole[...].reshape(width, width)

    for store in stores:
        store.wait()
    for copy in waits:
        copy.wait_send()
    for d in range(1, owners):
        copy, to_reducer = rs_copy(d)
        when(to_reducer)(copy.wait_send)

    def sent():
        hop.wait_send()
        for d in range(1, owners):
            ag_copy(d).wait_send()

    when(i_reduce)(sent)


def travel(start, blocks, cols, counts):
    block_rows, slots, tile, _ = blocks.shape
    rows_here, width = start.shape
    phases, owners = lax.axis_size("phase"), lax.axis_size("rows")
    panels = width // LANES
    rim = HB * tile
    reducers = min(owners, width // 32)
    share = width // reducers
    part_count = 3 if rows_here > 2 * rim else 2
    dma = pltpu.SemaphoreType.DMA
    vmem = pl.BlockSpec(memory_space=pltpu.VMEM)
    smem = pl.BlockSpec(memory_space=pltpu.SMEM)
    anywhere = pl.BlockSpec(memory_space=pl.ANY)
    return pl.pallas_call(
        functools.partial(travel_kernel, phases, owners, reducers),
        out_shape=(
            jax.ShapeDtypeStruct((rows_here, width), jnp.bfloat16),
            jax.ShapeDtypeStruct((width, width), jnp.float32),
        ),
        in_specs=[anywhere, anywhere, smem, smem],
        out_specs=(anywhere, vmem),
        scratch_shapes=[
            pltpu.VMEM((block_rows, slots, tile, tile), jnp.bfloat16),
            pltpu.VMEM((block_rows, tile, (2 * HB + 1) * tile), jnp.bfloat16),
            pltpu.VMEM((phases + 1, panels, rows_here + 2 * rim, LANES), jnp.bfloat16),
            pltpu.VMEM((phases, panels, rows_here, LANES), jnp.bfloat16),
            pltpu.VMEM((reducers, share, width), jnp.bfloat16),
            pltpu.VMEM((owners, share, width), jnp.bfloat16),
            pltpu.VMEM((share, width), jnp.float32),
            pltpu.VMEM((share, width), jnp.float32),
            pltpu.VMEM((reducers, share, width), jnp.float32),
            dma((panels + 1,)),
            dma((phases, panels, 2)),
            dma((phases, panels, 2)),
            dma((phases, panels, part_count)),
            dma((phases, panels, part_count)),
            dma((owners,)),
            dma((owners,)),
            dma((1,)),
            dma((1,)),
            dma((owners,)),
            dma((owners,)),
        ],
        compiler_params=pltpu.CompilerParams(
            collective_id=0, has_side_effects=True, vmem_limit_bytes=62 * 1024 * 1024
        ),
        name="travel",
    )(start, blocks, cols, counts)


def ortho_kernel(
    panel, gram_ref, arrived_hbm, basis_hbm, factor_ref, upper, inverse, arrived_ref, basis_ref, load, store
):
    n = gram_ref.shape[0]
    leaf = 8
    fetch = pltpu.make_async_copy(arrived_hbm, arrived_ref, load.at[0])
    fetch.start()
    row_at = lax.broadcasted_iota(jnp.int32, (n, n), 0)
    col_at = lax.broadcasted_iota(jnp.int32, (n, n), 1)
    upper[...] = gram_ref[...]
    inverse[...] = jnp.where(row_at == col_at, 1.0, 0.0).astype(jnp.float32)
    at_row = lax.broadcasted_iota(jnp.int32, (leaf, LANES), 0)

    for first in range(0, n, panel):
        lo = first // LANES * LANES
        hi = ((first + panel - 1) // LANES + 1) * LANES
        places = [(upper, t) for t in range(lo, n, LANES)] + [(inverse, t) for t in range(0, hi, LANES)]
        rest = [ref[first : first + panel, t : t + LANES] for ref, t in places]
        for base in range(first, first + panel, leaf):
            left = first + panel - base - leaf
            heads = [x[:leaf] for x in rest]
            tails = [x[leaf:] for x in rest] if left else []
            pick = base % LANES
            source = (base // LANES * LANES - lo) // LANES
            col_head = [
                jnp.broadcast_to(heads[source][:, pick + j : pick + j + 1], (leaf, LANES)) for j in range(leaf)
            ]
            col_tail = [
                jnp.broadcast_to(tails[source][:, pick + j : pick + j + 1], (left, LANES)) for j in range(leaf)
            ] if left else []
            for k in range(leaf):
                scale = lax.rsqrt(col_head[k][k : k + 1, :])
                low = col_head[k] * scale
                low_tail = col_tail[k] * scale if left else None
                for j in range(k + 1, leaf):
                    by = low[j : j + 1, :]
                    col_head[j] = col_head[j] - low * by
                    if left:
                        col_tail[j] = col_tail[j] - low_tail * by
                masked = jnp.where(at_row > k, low, 0.0)
                for t in range(len(places)):
                    row = heads[t][k : k + 1, :] * scale
                    heads[t] = jnp.where(at_row == k, row, heads[t] - masked * row)
                    if left:
                        tails[t] = tails[t] - low_tail * row
            for (ref, t), head in zip(places, heads):
                ref[base : base + leaf, t : t + LANES] = head
            rest = tails
        done = first + panel
        if done < n:
            start = done // LANES * LANES
            solved = upper[first:done, start:]
            contract = (((0,), (0,)), ((), ()))
            for ref, a, b in ((upper, start, n), (inverse, 0, hi)):
                change = lax.dot_general(
                    solved, ref[first:done, a:b], contract,
                    precision=lax.Precision.HIGHEST, preferred_element_type=jnp.float32,
                )
                ref[done:, a:b] = ref[done:, a:b] - change[done - start :]
    factor_ref[...] = jnp.where(col_at >= row_at, upper[...], 0.0)
    weights = inverse[...]
    coarse = weights.astype(jnp.bfloat16)
    fine = (weights - coarse.astype(jnp.float32)).astype(jnp.bfloat16)
    contract = (((1,), (1,)), ((), ()))
    step = n
    fetch.wait()
    writes = []
    for at in range(0, arrived_ref.shape[0], step):
        rows = arrived_ref[at : at + step, :]
        basis_ref[at : at + step, :] = lax.dot_general(
            rows, coarse, contract, preferred_element_type=jnp.float32
        ) + lax.dot_general(rows, fine, contract, preferred_element_type=jnp.float32)
        write = pltpu.make_async_copy(
            basis_ref.at[pl.ds(at, step), :], basis_hbm.at[pl.ds(at, step), :], store.at[at // step]
        )
        write.start()
        writes.append(write)
    for write in writes:
        write.wait()


def ortho(gram, arrived, panel=64):
    n = gram.shape[0]
    vmem = pl.BlockSpec(memory_space=pltpu.VMEM)
    return pl.pallas_call(
        functools.partial(ortho_kernel, panel),
        out_shape=(
            jax.ShapeDtypeStruct(arrived.shape, jnp.float32),
            jax.ShapeDtypeStruct((n, n), jnp.float32),
        ),
        in_specs=[vmem, pl.BlockSpec(memory_space=pl.ANY)],
        out_specs=(pl.BlockSpec(memory_space=pl.ANY), vmem),
        scratch_shapes=[
            pltpu.VMEM((n, n), jnp.float32),
            pltpu.VMEM((n, n), jnp.float32),
            pltpu.VMEM(arrived.shape, jnp.bfloat16),
            pltpu.VMEM(arrived.shape, jnp.float32),
            pltpu.SemaphoreType.DMA((1,)),
            pltpu.SemaphoreType.DMA((arrived.shape[0] // n,)),
        ],
        compiler_params=pltpu.CompilerParams(vmem_limit_bytes=62 * 1024 * 1024),
        name="ortho",
    )(gram, arrived)


def body(start, blocks, cols, counts):
    arrived, gram = travel(start[0], blocks[0], cols[0], counts[0])
    basis, factor = ortho(gram, arrived)
    return (basis[None], factor[None])


def solution(mesh):
    placed = (
        P("phase", "rows", None),
        P("phase", "rows", None, None, None),
        P("phase", "rows", None),
        P("phase", "rows"),
    )
    return jax.shard_map(
        body,
        mesh=mesh,
        in_specs=placed,
        out_specs=(P("phase", "rows", None), P("phase", None, None)),
        check_vma=False,
    )
```
